512 devices in a mesh: rep: 16 (over y, core), tp: 8 (over x, z_lo), fsdp: 4 (over z_hi).
Axes of the slice: x: 4, y: 8, z: 8 (z_hi: 4, z_lo: 2; z = z_hi * 2 + z_lo), core: 2. Of those that a mesh axis runs over, the one named last changes fastest.
Arguments:
- hidden_in: bfloat16 [65536, 5120], P(('rep', 'fsdp'), 'tp'), may hold values from -6 to 6
- target_rows: bfloat16 [65536, 5120], P(('rep', 'fsdp'), 'tp'), may hold values from -0.078125 to 0.078125
- grads: float32 [5120, 5120], P(('rep', 'fsdp'), 'tp')
- master: float32 [5120, 5120], P(('rep', 'fsdp'), 'tp'), may hold values from -0.078125 to 0.078125
- first_moment: float32 [5120, 5120], P(('rep', 'fsdp'), 'tp'), may hold values from -0.0012 to 0.0012
- second_moment: float32 [5120, 5120], P(('rep', 'fsdp'), 'tp'), may hold values from 1e-09 to 1e-07
- ref_weight: bfloat16 [5120, 5120], P(('rep', 'fsdp'), 'tp'), may hold values from -0.078125 to 0.078125
- lengths: int32 [64], P(('rep', 'fsdp')), may hold values from 768 to 1024, as said below
- boundaries: int32 [64, 8], P(('rep', 'fsdp')), may hold values from 1 to 1023, as said below
Outputs:
- step_rewards: float32 [64, 9], P(('rep', 'fsdp'))
- master_new: float32 [5120, 5120], P(('rep', 'fsdp'), 'tp')
- moment_one: float32 [5120, 5120], P(('rep', 'fsdp'), 'tp')
- moment_two: float32 [5120, 5120], P(('rep', 'fsdp'), 'tp')
The draws below stay inside these ranges and needn't reach their ends.
Inputs may be any that keep to these rules, and one draw needn't show every extreme that they name: lengths lie between 768 and 1024; some rollout has length 1024. boundaries of a rollout rise strictly and stay below its length.
All inputs are finite; a program needn't handle non-finite values.
Results may differ from the reference program's by a relative error of at most 0.0031.
Values may be sent and summed in bfloat16 or wider, within the bound.
A program may use at most 64 MiB of HBM per device.

```python
import math
import jax
import jax.numpy as jnp
from jax import lax

D = 5120
LEN = 1024
STEPS = 8
ROLLOUTS = 64
TOKENS = 65536


def shared_bounds(key):
    key_len, key_jit = jax.random.split(key)
    short = jax.random.randint(key_len, (ROLLOUTS,), 0, LEN // 4 + 1)
    short = short.at[0].set(0)
    length = LEN - short
    jitter_max = LEN // (4 * (STEPS + 1))
    jitter = jax.random.randint(key_jit, (ROLLOUTS, STEPS), -jitter_max, jitter_max + 1)
    index = jnp.arange(1, STEPS + 1, dtype=jnp.int32)
    ends = length[:, None] * index[None, :] // (STEPS + 1) + jitter
    return (length.astype(jnp.int32), ends.astype(jnp.int32))


def draw_lengths(key, part):
    length, ends = shared_bounds(key)
    return length


def draw_boundaries(key, part):
    length, ends = shared_bounds(key)
    return ends


def draw_grads(key, part):
    key = jax.random.fold_in(key, 7)
    key_n, key_r, key_c = jax.random.split(key, 3)
    rows = jnp.arange(D, dtype=jnp.float32)[:, None] / D
    rise = jnp.exp(jnp.log(3.0) * rows)
    row_scale = jnp.exp(jax.random.uniform(key_r, (D, 1), jnp.float32, 0.0, jnp.log(10.0)))
    col_scale = jnp.exp(jax.random.uniform(key_c, (1, D), jnp.float32, 0.0, jnp.log(10.0)))
    base = jax.random.normal(key_n, (D, D), jnp.float32)
    return base * rise * row_scale * col_scale


def block_scale(key, dims, pieces, least, high):
    loudness = 1.0
    for axis_at, shards_of in pieces:
        heights = jax.random.uniform(jax.random.fold_in(jax.random.fold_in(key, 6), axis_at), (shards_of,), jnp.float32, least / len(pieces), high / len(pieces))
        loudness = loudness * jnp.repeat(jnp.exp(heights), dims[axis_at] // shards_of).reshape((-1,) + (1,) * (len(dims) - 1 - axis_at))
    return loudness


def scatter_about(own_key, extent, width, bound, pieces=(), kind=jnp.bfloat16):
    loudness = block_scale(own_key, extent, pieces, -0.22, 0.18) if pieces else 1.0
    drawn = jax.random.normal(own_key, extent, jnp.float32) * width * loudness
    return jnp.minimum(jnp.maximum(drawn, -bound), bound).astype(kind)


def setup_inputs(seed: int = 0) -> dict:
    streams_of = jax.random.split(jax.random.key(seed), 10)
    return {
        "hidden_in": scatter_about(streams_of[0], (TOKENS, D), 1.0, 6.0, ((0, 64), (1, 8))),
        "target_rows": scatter_about(streams_of[1], (TOKENS, D), D ** -0.5, 0.078125, ((0, 64), (1, 8))),
        "grads": draw_grads(jax.random.fold_in(streams_of[9], 71), 0),
        "master": scatter_about(streams_of[3], (D, D), D ** -0.5, 0.078125, ((0, 64), (1, 8)), jnp.float32),
        "first_moment": scatter_about(streams_of[4], (D, D), 0.0002, 0.0012, ((0, 64), (1, 8)), jnp.float32),
        "second_moment": jnp.clip(jnp.exp(math.log(1.0000000116860974e-07) - 4.6051702 * jax.random.uniform(streams_of[5], (D, D), jnp.float32) ** block_scale(streams_of[5], (D, D), ((0, 64), (1, 8)), -0.2, 0.2)), 9.999999717180685e-10, 1.0000000116860974e-07),
        "ref_weight": scatter_about(streams_of[6], (D, D), D ** -0.5, 0.078125, ((0, 64), (1, 8))),
        "lengths": draw_lengths(jax.random.fold_in(streams_of[9], 71), 0),
        "boundaries": draw_boundaries(jax.random.fold_in(streams_of[9], 71), 0),
    }


first_fix = 1.0 - (0.9 ** 10) ** 10
second_fix = 1.0 - (0.95 ** 10) ** 10

def reference(hidden_in, target_rows, grads, master, first_moment, second_moment, ref_weight, lengths, boundaries):
    grad_norm = jnp.sqrt(jnp.sum(grads * grads) + 1e-06)
    clip = 1.0 / grad_norm
    scaled = clip * grads
    moment_one = 0.9 * first_moment + 0.1 * scaled
    moment_two = 0.95 * second_moment + 0.05 * scaled * scaled
    corrected = moment_one / first_fix / (jnp.sqrt(moment_two / second_fix) + 1e-08)
    master_new = master - 0.002 * (corrected + 0.1 * master)
    delta = (master_new - ref_weight.astype(jnp.float32)).astype(jnp.bfloat16)
    proj = jnp.dot(hidden_in, delta, preferred_element_type=jnp.float32)
    score = 0.05 * lax.optimization_barrier(jnp.sum(proj * target_rows.astype(jnp.float32), axis=1))
    score = score.reshape(ROLLOUTS, LEN)
    position = jnp.arange(LEN, dtype=jnp.int32)
    step_of = lax.optimization_barrier(jnp.sum((position[None, :, None] >= boundaries[:, None, :]).astype(jnp.int32), axis=-1))
    live = position[None, :] < lengths[:, None]
    onehot = ((step_of[:, :, None] == jnp.arange(STEPS + 1, dtype=jnp.int32)[None, None, :]) & live[:, :, None]).astype(jnp.float32)
    step_rewards = lax.optimization_barrier(jnp.sum(score[:, :, None] * onehot, axis=1))
    return (step_rewards, master_new, moment_one, moment_two)
```

```python
import functools

import jax
import jax.numpy as jnp
from jax import lax
from jax.experimental import pallas as pl
from jax.experimental.pallas import tpu as pltpu
from jax.sharding import PartitionSpec as P

MESH = pl.DeviceIdType.MESH
STEPS = 8
NX, NY, NZ = 4, 8, 4
UNIT = (0, 1, 3, 2)
HALF = ((0, 2), (1, 3))

first_fix = 1.0 - (0.9**10) ** 10
second_fix = 1.0 - (0.95**10) ** 10


def kernel(
    hidden, target, grads, master, first, second, refw, lengths, bounds,
    steps_out, master_out, first_out, second_out,
    hid, tgt, dlt, piece, g_v, ma_v, m1_v, m2_v, rw_v, mo_v, o1_v, o2_v,
    na, nb, nc, sums, score,
    local_sem, out_sem,
    na_s, na_r, nb_s, nb_r, nc_s, nc_r, su_s, su_r,
    x_s, x_r, t_s, t_r, z_s, z_r, y_s, y_r, c_s, c_r,
):
    rep, tp, z = lax.axis_index("rep"), lax.axis_index("tp"), lax.axis_index("fsdp")
    y, core = rep // 2, rep % 2
    x, zl = tp // 2, tp % 2
    nrep, ntp = 2 * NY, 2 * NX
    rows = piece.shape[0]
    tokens = hid.shape[1]
    chunk = tokens // 4
    is_source = zl == y % 2

    def remote(src, dst, send, recv, device):
        return pltpu.make_async_remote_copy(
            src_ref=src, dst_ref=dst, send_sem=send, recv_sem=recv,
            device_id=device, device_id_type=MESH,
        )

    loads = [
        pltpu.make_async_copy(a, b, local_sem.at[i])
        for i, (a, b) in enumerate((
            (grads, g_v),
            (hidden, hid.at[x]),
            (first, m1_v),
            (second, m2_v),
            (master, ma_v),
            (refw, rw_v),
            (target, tgt.at[zl]),
        ))
    ]
    for c in loads:
        c.start()

    barrier = pltpu.get_barrier_semaphore()

    def greet(device):
        pl.semaphore_signal(barrier, inc=1, device_id=device, device_id_type=MESH)

    for r in range(1, nrep):
        greet(((rep + r) % nrep, tp, z))
    for r in range(1, ntp):
        greet((rep, (tp + r) % ntp, z))
    for r in range(1, NZ):
        greet((rep, tp, (z + r) % NZ))
        greet((rep, x * 2 + 1 - zl, (z + r) % NZ))

    loads[0].wait()
    g = g_v[...]
    sq = g * g
    part = jnp.sum(jnp.sum(sq, axis=0, keepdims=True), axis=1, keepdims=True)
    na[tp] = jnp.broadcast_to(part, (8, 128))
    pl.semaphore_wait(barrier, nrep - 1 + ntp - 1 + 2 * (NZ - 1))

    def spread(buf, me, n, sends, recv, device_of):
        out = []
        for r in range(1, n):
            c = remote(buf.at[me], buf.at[me], sends.at[r - 1], recv, device_of((me + r) % n))
            c.start()
            out.append(c)
        return out

    def gather_wait(buf, n, sends, recv):
        part = buf.at[pl.ds(0, n - 1)]
        remote(part, part, sends.at[0], recv, (rep, tp, z)).wait_recv()

    pending = []
    pending += spread(na, tp, ntp, na_s, na_r, lambda j: (rep, j, z))

    gather_wait(na, ntp, na_s, na_r)
    nb[rep] = jnp.sum(na[...], axis=0)
    pending += spread(nb, rep, nrep, nb_s, nb_r, lambda j: (j, tp, z))

    xp = (rep, ((x + 1) % NX) * 2 + zl, z)
    xm = (rep, ((x + NX - 1) % NX) * 2 + zl, z)
    loads[1].wait()

    def x_copy(d, k, owner, c):
        ref = hid.at[owner, pl.ds(c * chunk, chunk)]
        return remote(ref, ref, x_s.at[d, k], x_r.at[d, k], (xp, xm)[d])

    for i in range(4):
        for d, c in ((0, i), (1, (i + 2) % 4)):
            copy = x_copy(d, c, x, c)
            copy.start()
            pending.append(copy)

    gather_wait(nb, nrep, nb_s, nb_r)
    nc[z] = jnp.sum(nb[...], axis=0)
    pending += spread(nc, z, NZ, nc_s, nc_r, lambda j: (rep, tp, j))
    for c in loads[2:]:
        c.wait()
    gather_wait(nc, NZ, nc_s, nc_r)
    total = jnp.sum(nc[...], axis=0)[0:1, 0:1]
    clip = 1.0 / jnp.sqrt(total + 1e-06)

    scaled = clip * g_v[...]
    moment_one = 0.9 * m1_v[...] + 0.1 * scaled
    moment_two = 0.95 * m2_v[...] + 0.05 * scaled * scaled
    corrected = moment_one / first_fix / (jnp.sqrt(moment_two / second_fix) + 1e-08)
    old = ma_v[...]
    master_new = old - 0.002 * (corrected + 0.1 * old)
    delta = (master_new - rw_v[...].astype(jnp.float32)).astype(jnp.bfloat16)
    piece[...] = delta
    mo_v[...] = master_new
    o1_v[...] = moment_one
    o2_v[...] = moment_two

    def at(z_o, core_o):
        return pl.ds(pl.multiple_of((core_o * NZ + z_o) * rows, 16), rows)

    @pl.when(is_source)
    def _():
        dlt[y // 2, zl, at(z, core)] = delta

    def z_copy(r):
        return remote(
            piece, dlt.at[y // 2, zl, at(z, core)], z_s.at[r], z_r.at[z, zl],
            (rep, x * 2 + y % 2, (z + r) % NZ),
        )

    @pl.when(jnp.logical_not(is_source))
    def _():
        z_copy(0).start()

    for r in (1, 3, 2):
        z_copy(r).start()

    outs = [
        pltpu.make_async_copy(a, b, out_sem.at[i])
        for i, (a, b) in enumerate(((mo_v, master_out), (o1_v, first_out), (o2_v, second_out)))
    ]
    for c in outs:
        c.start()

    def t_copy(owner, c):
        ref = tgt.at[owner, pl.ds(c * chunk, chunk)]
        return remote(ref, ref, t_s.at[c], t_r.at[c], (rep, x * 2 + 1 - zl, z))

    for c in range(4):
        copy = t_copy(zl, c)
        copy.start()
        pending.append(copy)

    def x_relay(i):
        x_copy(0, i, (x + NX - 1) % NX, i).wait_recv()
        x_copy(0, 4 + i, (x + NX - 1) % NX, i).start()
        x_copy(1, 2 + i, (x + 1) % NX, 2 + i).wait_recv()
        x_copy(1, 4 + i, (x + 1) % NX, 2 + i).start()

    yp = (((y + 1) % NY) * 2 + core, tp, z)
    ym = (((y + NY - 1) % NY) * 2 + core, tp, z)
    other = (rep + 1 - 2 * core, tp, z)

    def unit(y_o, u, core_o):
        return dlt.at[(y_o + 2 * NY) % NY // 2, :, at((z + UNIT[u]) % NZ, core_o)]

    def y_copy(d, k, y_o, u):
        ref = unit(y_o, u, core)
        return remote(ref, ref, y_s.at[d, k], y_r.at[d, k], (yp, ym)[d])

    def c_copy(y_o, u, core_o):
        a = (y_o + 2 * NY) % NY // 2
        ref = unit(y_o, u, core_o)
        return remote(ref, ref, c_s.at[a, u], c_r.at[a, u], other)

    def origin(source, d, k):
        far = (4 if source else 3) if k >= 4 else (2 if source else 1)
        u = k if k < 4 else (HALF[d][k - 4] if source else k - 4)
        return (y - far if d == 0 else y + far), u

    def take(source, d, k):
        y_o, u = origin(source, d, k)
        y_copy(d, k, y_o, u).wait_recv()
        if k < 4:
            y_copy(d, k + (4 if source else 0), y_o, u).start()
        elif not source and u in HALF[d]:
            y_copy(d, 4 + HALF[d].index(u), y_o, u).start()
        c_copy(y_o, u, core).start()

    @pl.when(is_source)
    def _():
        for u in range(4):
            z_o = (z + UNIT[u]) % NZ
            for b in range(2):
                ref = dlt.at[y // 2, b, at(z_o, core)]
                arrival = remote(ref, ref, z_s.at[0], z_r.at[z_o, b], (rep, tp, z))
                if u == 0:
                    pl.when(b != zl)(lambda a=arrival: a.wait_recv())
                else:
                    arrival.wait_recv()
            y_copy(0, u, y, u).start()
            y_copy(1, u, y, u).start()
            c_copy(y, u, core).start()
        for k in range(6):
            if k in (1, 3):
                x_relay(k // 2)
            take(True, 0, k)
            take(True, 1, k)

    @pl.when(jnp.logical_not(is_source))
    def _():
        for k in range(8):
            if k in (2, 4):
                x_relay(k // 2 - 1)
            take(False, 0, k)
            take(False, 1, k)

    for c in range(4):
        t_copy(1 - zl, c).wait_recv()
    for k in range(4):
        if k >= 2:
            x_copy(0, k, (x + NX - 1) % NX, k).wait_recv()
        if k < 2:
            x_copy(1, k, (x + 1) % NX, k).wait_recv()
    for k in range(4, 6):
        x_copy(0, k, (x + 2) % NX, k - 4).wait_recv()
        x_copy(1, k, (x + 2) % NX, k - 2).wait_recv()
    for a in range(NX):
        for u in range(4):
            c_copy(2 * a + zl, u, 1 - core).wait_recv()

    width = dlt.shape[-1]

    def tile(t, carry):
        at_t = pl.ds(pl.multiple_of(t * chunk, chunk), chunk)
        acc = jnp.zeros((chunk, 128), jnp.float32)
        for b in range(2):
            proj = jnp.zeros((chunk, width), jnp.float32)
            for a in range(NX):
                proj += jnp.dot(hid[a, at_t], dlt[a, b], preferred_element_type=jnp.float32)
            prod = proj * tgt[b, at_t].astype(jnp.float32)
            for j in range(width // 128):
                acc += prod[:, j * 128 : (j + 1) * 128]
        score[at_t] = acc
        return carry

    lax.fori_loop(0, 4, tile, 0)

    lane = lax.broadcasted_iota(jnp.int32, (1, 128), 1)
    low = jnp.zeros((1, 128), jnp.int32)
    high = jnp.where(lane == STEPS, lengths[0], jnp.zeros((1, 128), jnp.int32))
    for k in range(STEPS):
        low = jnp.where(lane == k + 1, bounds[0, k], low)
        high = jnp.where(lane == k, jnp.minimum(bounds[0, k], lengths[0]), high)
    pos = lax.broadcasted_iota(jnp.int32, (tokens, 128), 0)
    inside = (pos >= low) & (pos < high)
    line = jnp.sum(score[...], axis=1, keepdims=True)
    part = 0.05 * jnp.sum(jnp.where(inside, line, 0.0), axis=0, keepdims=True)
    sums[tp] = jnp.broadcast_to(part, (8, 128))
    pending += spread(sums, tp, ntp, su_s, su_r, lambda j: (rep, j, z))
    gather_wait(sums, ntp, su_s, su_r)
    steps_out[...] = jnp.sum(sums[...], axis=0)[0:1, 0 : STEPS + 1]

    for c in pending:
        c.wait_send()
    for i in range(2):
        x_copy(0, 4 + i, (x + NX - 1) % NX, i).wait_send()
        x_copy(1, 4 + i, (x + 1) % NX, 2 + i).wait_send()
    for r in range(1, 4):
        z_copy(r).wait_send()
    for a in range(NX):
        for u in range(4):
            c_copy(2 * a + zl, u, core).wait_send()
    for d in range(2):
        for k in range(6):
            y_copy(d, k, y, 0).wait_send()

    @pl.when(is_source)
    def _():
        for d in range(2):
            for k in range(6, 8):
                y_copy(d, k, y, 0).wait_send()

    @pl.when(jnp.logical_not(is_source))
    def _():
        z_copy(0).wait_send()

    for c in outs:
        c.wait()


def local(hidden_in, target_rows, grads, master, first_moment, second_moment, ref_weight, lengths, boundaries):
    tokens, width = hidden_in.shape
    rows = grads.shape[0]
    f32, bf16 = jnp.float32, jnp.bfloat16
    weight = jax.ShapeDtypeStruct(grads.shape, f32)
    dma, vmem = pltpu.SemaphoreType.DMA, pltpu.VMEM
    any_space = pl.BlockSpec(memory_space=pl.ANY)
    smem = pl.BlockSpec(memory_space=pltpu.SMEM)
    return tuple(
        pl.pallas_call(
            kernel,
            out_shape=(jax.ShapeDtypeStruct((1, STEPS + 1), f32), weight, weight, weight),
            in_specs=[any_space] * 7 + [smem] * 2,
            out_specs=(pl.BlockSpec(memory_space=pltpu.VMEM), any_space, any_space, any_space),
            scratch_shapes=[
                vmem((NX, tokens, width), bf16),
                vmem((2, tokens, width), bf16),
                vmem((NX, 2, 8 * rows, width), bf16),
                vmem((rows, width), bf16),
                *[vmem((rows, width), f32)] * 4,
                vmem((rows, width), bf16),
                *[vmem((rows, width), f32)] * 3,
                vmem((2 * NX, 8, 128), f32),
                vmem((2 * NY, 8, 128), f32),
                vmem((NZ, 8, 128), f32),
                vmem((2 * NX, 8, 128), f32),
                vmem((tokens, 128), f32),
                dma((7,)),
                dma((3,)),
                dma((2 * NX - 1,)), dma(()),
                dma((2 * NY - 1,)), dma(()),
                dma((NZ - 1,)), dma(()),
                dma((2 * NX - 1,)), dma(()),
                dma((2, 6)), dma((2, 6)),
                dma((4,)), dma((4,)),
                dma((4,)), dma((4, 2)),
                dma((2, 8)), dma((2, 8)),
                dma((4, 4)), dma((4, 4)),
            ],
            compiler_params=pltpu.CompilerParams(
                collective_id=0, has_side_effects=True, vmem_limit_bytes=48 * 2**20
            ),
            cost_estimate=pl.CostEstimate(
                flops=2 * tokens * 8 * width * width, bytes_accessed=6 * 2**20, transcendentals=0
            ),
        )(hidden_in, target_rows, grads, master, first_moment, second_moment, ref_weight, lengths, boundaries)
    )


def solution(mesh):
    block = P(("rep", "fsdp"), "tp")
    return jax.shard_map(
        local,
        mesh=mesh,
        in_specs=(block,) * 7 + (P(("rep", "fsdp")), P(("rep", "fsdp"), None)),
        out_specs=(P(("rep", "fsdp"), None), block, block, block),
        check_vma=False,
    )
```

```python
import functools

import jax
import jax.numpy as jnp
from jax import lax
from jax.experimental import pallas as pl
from jax.experimental.pallas import tpu as pltpu
from jax.sharding import PartitionSpec as P

MESH = pl.DeviceIdType.MESH
STEPS = 8
NX, NY, NZ = 4, 8, 4
NEAR = ((0, 1, 2, 3), (0, 2, 3, 1))
FAR = ((0, 1, 2, 3), (1, 2, 0, 3))


first_fix = 1.0 - (0.9**10) ** 10
second_fix = 1.0 - (0.95**10) ** 10


def kernel(
    hidden, target, grads, master, first, second, refw, lengths, bounds,
    total_out, sums_out,
    hid, tgt, dlt, piece, g_v, ma_v, m1_v, m2_v, rw_v,
    na, nb, nc, sums, score,
    local_sem,
    na_s, na_r, nb_s, nb_r, nc_s, nc_r, su_s, su_r,
    x_s, x_r, t_s, t_r, z_s, z_r, y_s, y_r, c_s, c_r,
):
    rep, tp, z = lax.axis_index("rep"), lax.axis_index("tp"), lax.axis_index("fsdp")
    y, core = rep // 2, rep % 2
    x, zl = tp // 2, tp % 2
    ntp = 2 * NX
    rows = piece.shape[0]
    tokens = hid.shape[1]
    half = tokens // 2
    chunk = tokens // 4
    is_source = zl == y % 2
    not_source = jnp.logical_not(is_source)

    def remote(src, dst, send, recv, device):
        return pltpu.make_async_remote_copy(
            src_ref=src, dst_ref=dst, send_sem=send, recv_sem=recv,
            device_id=device, device_id_type=MESH,
        )

    width = piece.shape[1]

    def half_of(b):
        return pl.ds(pl.multiple_of(b * width, 128), width)

    loads = [
        pltpu.make_async_copy(a, b, local_sem.at[i])
        for i, (a, b) in enumerate((
            (grads, g_v),
            (hidden, hid.at[x]),
            (first, m1_v),
            (second, m2_v),
            (master, ma_v),
            (refw, rw_v),
            (target, tgt.at[:, half_of(zl)]),
        ))
    ]
    for c in loads:
        c.start()

    barrier = pltpu.get_barrier_semaphore()

    def in_tp(j):
        return rep, j, z

    def in_y(j):
        return j * 2 + core, tp, z

    def in_cz(j):
        return y * 2 + j // NZ, tp, j % NZ

    def greet(device):
        pl.semaphore_signal(barrier, inc=1, device_id=device, device_id_type=MESH)

    cz = core * NZ + z
    for r in range(1, 8):
        greet(in_tp((tp + r) % 8))
        greet(in_y((y + r) % 8))
        greet(in_cz((cz + r) % 8))
    for r in range(1, NZ):
        greet((rep, x * 2 + 1 - zl, (z + r) % NZ))

    loads[0].wait()
    g = g_v[...]
    part = jnp.sum(jnp.sum(g * g, axis=0, keepdims=True), axis=1, keepdims=True)
    na[tp, 0:1] = jnp.broadcast_to(part, (1, 128))
    pl.semaphore_wait(barrier, 3 * 7 + NZ - 1)

    def spread(buf, me, sends, recv, device_of):
        out = []
        row = buf.at[me, pl.ds(0, 1)]
        for r in range(1, 8):
            c = remote(row, row, sends.at[r - 1], recv, device_of((me + r) % 8))
            c.start()
            out.append(c)
        return out

    def gather(buf, sends, recv):
        part = buf.at[pl.ds(0, 7), pl.ds(0, 1)]
        remote(part, part, sends.at[0], recv, (rep, tp, z)).wait_recv()
        return jnp.sum(buf[:, 0:1, :], axis=0)

    xp = (rep, ((x + 1) % NX) * 2 + zl, z)
    xm = (rep, ((x + NX - 1) % NX) * 2 + zl, z)

    def x_copy(d, k, owner, c):
        ref = hid.at[owner, pl.ds(c * half, half)]
        return remote(ref, ref, x_s.at[d, k], x_r.at[d, k], (xp, xm)[d])

    def x_relay():
        x_copy(0, 0, (x + NX - 1) % NX, 0).wait_recv()
        x_copy(0, 2, (x + NX - 1) % NX, 0).start()
        x_copy(1, 0, (x + 1) % NX, 1).wait_recv()
        x_copy(1, 2, (x + 1) % NX, 1).start()

    def t_copy(owner):
        ref = tgt.at[:, half_of(owner)]
        return remote(ref, ref, t_s, t_r, (rep, x * 2 + 1 - zl, z))

    pending = []

    def start(copy):
        copy.start()
        pending.append(copy)

    pending += spread(na, tp, na_s, na_r, in_tp)
    nb[y, 0:1] = gather(na, na_s, na_r)
    pending += spread(nb, y, nb_s, nb_r, in_y)

    loads[1].wait()
    for i in range(2):
        start(x_copy(0, i, x, i))
        start(x_copy(1, i, x, 1 - i))

    nc[cz, 0:1] = gather(nb, nb_s, nb_r)
    pending += spread(nc, cz, nc_s, nc_r, in_cz)
    score[...] = jnp.zeros_like(score)
    for c in loads[2:]:
        c.wait()
    total = gather(nc, nc_s, nc_r)
    total_out[...] = total
    total = total[:, 0:1]
    clip = 1.0 / jnp.sqrt(total + 1e-06)

    scaled = clip * g_v[...]
    moment_one = 0.9 * m1_v[...] + 0.1 * scaled
    moment_two = 0.95 * m2_v[...] + 0.05 * scaled * scaled
    corrected = moment_one / first_fix / (jnp.sqrt(moment_two / second_fix) + 1e-08)
    old = ma_v[...]
    master_new = old - 0.002 * (corrected + 0.1 * old)
    delta = (master_new - rw_v[...].astype(jnp.float32)).astype(jnp.bfloat16)
    piece[...] = delta

    def at(z_o, core_o):
        return pl.ds(pl.multiple_of((core_o * NZ + z_o) * rows, 16), rows)

    z_of = (z, z + 1 - 2 * (z % 2), NZ - 1 - z, (z + 2) % NZ)

    def z_copy(u):
        return remote(
            piece, dlt.at[y // 2, at(z, core), half_of(zl)], z_s.at[u], z_r.at[z, zl],
            (rep, x * 2 + y % 2, z_of[u]),
        )

    yp = in_y((y + 1) % NY)
    ym = in_y((y + NY - 1) % NY)
    other = (rep + 1 - 2 * core, tp, z)

    def unit(y_o, u, core_o):
        return dlt.at[(y_o + 2 * NY) % NY // 2, at(z_of[u], core_o)]

    def y_copy(d, k, y_o, u):
        ref = unit(y_o, u, core)
        return remote(ref, ref, y_s.at[d, k], y_r.at[d, k], (yp, ym)[d])

    def c_copy(y_o, pair, core_o):
        a = (y_o + 2 * NY) % NY // 2
        low = (core_o * 2 + (z // 2 + pair) % 2) * 2 * rows
        ref = dlt.at[a, pl.ds(pl.multiple_of(low, 16), 2 * rows)]
        return remote(ref, ref, c_s.at[a, pair], c_r.at[a, pair], other)

    def across(d, y_o, seen):
        if len(seen) >= 2:
            pair = seen[-1] // 2
            if {2 * pair, 2 * pair + 1} <= set(seen):
                c_copy(y_o, pair, core).start()

    def origin(d, hops):
        return y - hops if d == 0 else y + hops

    base = jnp.where(is_source, y // 2, (y + NY - 1) % NY // 2)
    turn = jnp.where(is_source, 1, -1)

    def ready(a):
        for pair in range(2):
            c_copy(2 * a + zl, pair, 1 - core).wait_recv()
        away = (a - x + NX) % NX

        @pl.when(away == 3)
        def _():
            x_copy(0, 1, (x + NX - 1) % NX, 1).wait_recv()

        @pl.when(away == 1)
        def _():
            x_copy(1, 1, (x + 1) % NX, 0).wait_recv()

        @pl.when(away == 2)
        def _():
            x_copy(0, 2, (x + 2) % NX, 0).wait_recv()
            x_copy(1, 2, (x + 2) % NX, 1).wait_recv()

    def products(low, high):
        def one(p, carry):
            i, t = p // 4, p % 4
            step = jnp.where(i == 1, NX - turn, jnp.where(i == 2, NX + turn, jnp.where(i == 3, 2, 0)))
            a = (base + step) % NX
            pl.when(t == 0)(lambda: ready(a))
            at_t = pl.ds(pl.multiple_of(t * chunk, chunk), chunk)
            acc = score[at_t]
            proj = jnp.dot(hid[a, at_t], dlt[a], preferred_element_type=jnp.float32)
            prod = proj * tgt[at_t].astype(jnp.float32)
            for j in range(2 * width // 128):
                acc += prod[:, j * 128 : (j + 1) * 128]
            score[at_t] = acc
            return carry

        lax.fori_loop(low, high, one, 0)

    @pl.when(is_source)
    def _():
        for u in (1, 2, 3):
            z_copy(u).start()
        dlt[y // 2, at(z, core), half_of(zl)] = delta
        t_copy(zl).start()
        for u in range(4):
            for b in range(2):
                ref = dlt.at[y // 2, at(z_of[u], core), half_of(b)]
                arrival = remote(ref, ref, z_s.at[1], z_r.at[z_of[u], b], (rep, tp, z))
                if u == 0:
                    pl.when(b != zl)(lambda a=arrival: a.wait_recv())
                else:
                    arrival.wait_recv()
            y_copy(0, u, y, u).start()
            if u != 1:
                y_copy(1, NEAR[1].index(u), y, u).start()
        y_copy(1, 3, y, 1).start()
        for pair in range(2):
            c_copy(y, pair, core).start()
        seen = [[], []]
        for i in range(4):
            if i == 1:
                x_relay()
            for d in range(2):
                near = FAR[d][i]
                late = []
                while len(seen[d]) <= near:
                    k = len(seen[d])
                    y_copy(d, k, origin(d, 2), NEAR[d][k]).wait_recv()
                    seen[d].append(NEAR[d][k])
                    late.append(list(seen[d]))
                y_copy(d, 4 + i, origin(d, 2), NEAR[d][near]).start()
                for got in late:
                    across(d, origin(d, 2), got)
        t_copy(1 - zl).wait_recv()
        products(0, 4)
        for d in range(2):
            for k in (4, 5):
                y_copy(d, k, origin(d, 4), NEAR[d][FAR[d][k - 4]]).wait_recv()
            c_copy(origin(d, 4), d, core).start()
        products(4, 12)
        for d in range(2):
            for k in range(8):
                y_copy(d, k, y, 0).wait_send()

    @pl.when(not_source)
    def _():
        for u in range(4):
            z_copy(u).start()
        t_copy(zl).start()
        for k in range(8):
            if k == 2:
                x_relay()
            for d in range(2):
                order = NEAR[d] if k < 4 else [NEAR[d][n] for n in FAR[d]]
                y_o = origin(d, 1 if k < 4 else 3)
                y_copy(d, k, y_o, order[k % 4]).wait_recv()
                if k < 6:
                    y_copy(d, k, y_o, order[k % 4]).start()
                across(d, y_o, order[: k % 4 + 1])
            if k == 5:
                t_copy(1 - zl).wait_recv()
                products(0, 4)
            if k == 6:
                products(4, 8)
        for d in range(2):
            for k in range(6):
                y_copy(d, k, y, 0).wait_send()
        z_copy(0).wait_send()

    products(jnp.where(is_source, 12, 8), 16)

    lane = lax.broadcasted_iota(jnp.int32, (1, 128), 1)
    low = jnp.zeros((1, 128), jnp.int32)
    high = jnp.where(lane == STEPS, lengths[0], jnp.zeros((1, 128), jnp.int32))
    for k in range(STEPS):
        low = jnp.where(lane == k + 1, bounds[0, k], low)
        high = jnp.where(lane == k, jnp.minimum(bounds[0, k], lengths[0]), high)
    pos = lax.broadcasted_iota(jnp.int32, (tokens, 128), 0)
    inside = (pos >= low) & (pos < high)
    line = jnp.sum(score[...], axis=1, keepdims=True)
    sums[tp, 0:1] = 0.05 * jnp.sum(jnp.where(inside, line, 0.0), axis=0, keepdims=True)
    pending += spread(sums, tp, su_s, su_r, in_tp)
    sums_out[...] = gather(sums, su_s, su_r)

    for c in pending:
        c.wait_send()
    t_copy(zl).wait_send()
    x_copy(0, 2, (x + NX - 1) % NX, 0).wait_send()
    x_copy(1, 2, (x + 1) % NX, 1).wait_send()
    for u in (1, 2, 3):
        z_copy(u).wait_send()
    for a in range(NX):
        for pair in range(2):
            c_copy(2 * a + zl, pair, core).wait_send()


def finish(total, sums, grads, master, first, second, steps_out, master_out, first_out, second_out):
    clip = 1.0 / jnp.sqrt(total[:, 0:1] + 1e-06)
    scaled = clip * grads[...]
    moment_one = 0.9 * first[...] + 0.1 * scaled
    moment_two = 0.95 * second[...] + 0.05 * scaled * scaled
    corrected = moment_one / first_fix / (jnp.sqrt(moment_two / second_fix) + 1e-08)
    old = master[...]
    master_out[...] = old - 0.002 * (corrected + 0.1 * old)
    first_out[...] = moment_one
    second_out[...] = moment_two
    steps_out[...] = sums[:, 0 : STEPS + 1]


def local(hidden_in, target_rows, grads, master, first_moment, second_moment, ref_weight, lengths, boundaries):
    tokens, width = hidden_in.shape
    rows = grads.shape[0]
    f32, bf16 = jnp.float32, jnp.bfloat16
    weight = jax.ShapeDtypeStruct(grads.shape, f32)
    line = jax.ShapeDtypeStruct((1, 128), f32)
    dma, vmem = pltpu.SemaphoreType.DMA, pltpu.VMEM
    any_space = pl.BlockSpec(memory_space=pl.ANY)
    smem = pl.BlockSpec(memory_space=pltpu.SMEM)
    in_vmem = pl.BlockSpec(memory_space=pltpu.VMEM)
    total, sums = pl.pallas_call(
        kernel,
        out_shape=(line, line),
        in_specs=[any_space] * 7 + [smem] * 2,
        out_specs=(in_vmem, in_vmem),
        scratch_shapes=[
            vmem((NX, tokens, width), bf16),
            vmem((tokens, 2 * width), bf16),
            vmem((NX, 8 * rows, 2 * width), bf16),
            vmem((rows, width), bf16),
            *[vmem((rows, width), f32)] * 4,
            vmem((rows, width), bf16),
            *[vmem((8, 8, 128), f32)] * 4,
            vmem((tokens, 128), f32),
            dma((7,)),
            *[dma((7,)), dma(())] * 4,
            dma((2, 3)), dma((2, 3)),
            dma(()), dma(()),
            dma((4,)), dma((4, 2)),
            dma((2, 8)), dma((2, 8)),
            dma((4, 2)), dma((4, 2)),
        ],
        compiler_params=pltpu.CompilerParams(
            collective_id=0, has_side_effects=True, vmem_limit_bytes=63 * 2**20
        ),
        cost_estimate=pl.CostEstimate(
            flops=2 * tokens * 8 * width * width, bytes_accessed=6 * 2**20, transcendentals=0
        ),
    )(hidden_in, target_rows, grads, master, first_moment, second_moment, ref_weight, lengths, boundaries)
    return tuple(
        pl.pallas_call(
            finish,
            out_shape=(jax.ShapeDtypeStruct((1, STEPS + 1), f32), weight, weight, weight),
            in_specs=[in_vmem] * 6,
            out_specs=(in_vmem,) * 4,
        )(total, sums, grads, master, first_moment, second_moment)
    )


def solution(mesh):
    block = P(("rep", "fsdp"), "tp")
    return jax.shard_map(
        local,
        mesh=mesh,
        in_specs=(block,) * 7 + (P(("rep", "fsdp")), P(("rep", "fsdp"), None)),
        out_specs=(P(("rep", "fsdp"), None), block, block, block),
        check_vma=False,
    )
```

```python
import functools

import jax
import jax.numpy as jnp
from jax import lax
from jax.experimental import pallas as pl
from jax.experimental.pallas import tpu as pltpu
from jax.sharding import PartitionSpec as P

MESH = pl.DeviceIdType.MESH
STEPS = 8
NX, NY, NZ = 4, 8, 4
NEAR = ((0, 1, 2, 3), (0, 2, 3, 1))
FAR = ((0, 1, 2, 3), (1, 2, 0, 3))


first_fix = 1.0 - (0.9**10) ** 10
second_fix = 1.0 - (0.95**10) ** 10


def kernel(
    hidden, target, grads, master, first, second, refw, lengths, bounds,
    total_out, sums_out,
    hid, tgt, dlt, piece, g_v, ma_v, m1_v, m2_v, rw_v,
    na, nb, nc, sums, score,
    local_sem,
    na_s, na_r, nb_s, nb_r, nc_s, nc_r, su_s, su_r,
    x_s, x_r, t_s, t_r, z_s, z_r, y_s, y_r, c_s, c_r,
):
    rep, tp, z = lax.axis_index("rep"), lax.axis_index("tp"), lax.axis_index("fsdp")
    y, core = rep // 2, rep % 2
    x, zl = tp // 2, tp % 2
    ntp = 2 * NX
    rows = piece.shape[0]
    tokens = hid.shape[1]
    half = tokens // 2
    chunk = tokens // 4
    is_source = zl == y % 2
    not_source = jnp.logical_not(is_source)

    def remote(src, dst, send, recv, device):
        return pltpu.make_async_remote_copy(
            src_ref=src, dst_ref=dst, send_sem=send, recv_sem=recv,
            device_id=device, device_id_type=MESH,
        )

    width = piece.shape[1]

    def half_of(b):
        return pl.ds(pl.multiple_of(b * width, 128), width)

    loads = [
        pltpu.make_async_copy(a, b, local_sem.at[i])
        for i, (a, b) in enumerate((
            (grads, g_v),
            (hidden, hid.at[x]),
            (first, m1_v),
            (second, m2_v),
            (master, ma_v),
            (refw, rw_v),
            (target, tgt.at[:, half_of(zl)]),
        ))
    ]
    for c in loads:
        c.start()

    barrier = pltpu.get_barrier_semaphore()

    def in_tp(j):
        return rep, j, z

    def in_y(j):
        return j * 2 + core, tp, z

    def in_cz(j):
        return y * 2 + j // NZ, tp, j % NZ

    def greet(device):
        pl.semaphore_signal(barrier, inc=1, device_id=device, device_id_type=MESH)

    cz = core * NZ + z
    for r in range(1, 8):
        greet(in_tp((tp + r) % 8))
        greet(in_y((y + r) % 8))
        greet(in_cz((cz + r) % 8))
    for r in range(1, NZ):
        greet((rep, x * 2 + 1 - zl, (z + r) % NZ))

    loads[0].wait()
    g = g_v[...]
    part = jnp.sum(jnp.sum(g * g, axis=0, keepdims=True), axis=1, keepdims=True)
    na[tp, 0:1] = jnp.broadcast_to(part, (1, 128))
    pl.semaphore_wait(barrier, 3 * 7 + NZ - 1)

    def spread(buf, me, sends, recv, device_of):
        out = []
        row = buf.at[me, pl.ds(0, 1)]
        for r in range(1, 8):
            c = remote(row, row, sends.at[r - 1], recv, device_of((me + r) % 8))
            c.start()
            out.append(c)
        return out

    def gather(buf, sends, recv):
        part = buf.at[pl.ds(0, 7), pl.ds(0, 1)]
        remote(part, part, sends.at[0], recv, (rep, tp, z)).wait_recv()
        return jnp.sum(buf[:, 0:1, :], axis=0)

    xp = (rep, ((x + 1) % NX) * 2 + zl, z)
    xm = (rep, ((x + NX - 1) % NX) * 2 + zl, z)

    def x_copy(d, k, owner, c):
        ref = hid.at[owner, pl.ds(c * half, half)]
        return remote(ref, ref, x_s.at[d, k], x_r.at[d, k], (xp, xm)[d])

    def x_relay():
        x_copy(0, 0, (x + NX - 1) % NX, 0).wait_recv()
        x_copy(0, 2, (x + NX - 1) % NX, 0).start()
        x_copy(1, 0, (x + 1) % NX, 1).wait_recv()
        x_copy(1, 2, (x + 1) % NX, 1).start()

    def t_copy(owner, c):
        ref = tgt.at[pl.ds(pl.multiple_of(c * chunk, 16), chunk), half_of(owner)]
        return remote(ref, ref, t_s.at[c], t_r.at[c], (rep, x * 2 + 1 - zl, z))

    pending = []

    def start(copy):
        copy.start()
        pending.append(copy)

    pending += spread(na, tp, na_s, na_r, in_tp)
    loads[6].wait()
    nb[y, 0:1] = gather(na, na_s, na_r)
    pending += spread(nb, y, nb_s, nb_r, in_y)

    loads[1].wait()
    for i in range(2):
        start(x_copy(0, i, x, i))
        start(x_copy(1, i, x, 1 - i))

    nc[cz, 0:1] = gather(nb, nb_s, nb_r)
    pending += spread(nc, cz, nc_s, nc_r, in_cz)
    score[...] = jnp.zeros_like(score)
    for c in loads[2:6]:
        c.wait()
    total = gather(nc, nc_s, nc_r)
    total_out[...] = total
    total = total[:, 0:1]
    clip = 1.0 / jnp.sqrt(total + 1e-06)

    scaled = clip * g_v[...]
    moment_one = 0.9 * m1_v[...] + 0.1 * scaled
    moment_two = 0.95 * m2_v[...] + 0.05 * scaled * scaled
    corrected = moment_one / first_fix / (jnp.sqrt(moment_two / second_fix) + 1e-08)
    old = ma_v[...]
    master_new = old - 0.002 * (corrected + 0.1 * old)
    delta = (master_new - rw_v[...].astype(jnp.float32)).astype(jnp.bfloat16)
    piece[...] = delta

    def at(z_o, core_o):
        return pl.ds(pl.multiple_of((core_o * NZ + z_o) * rows, 16), rows)

    z_of = (z, z + 1 - 2 * (z % 2), NZ - 1 - z, (z + 2) % NZ)

    def z_copy(u):
        return remote(
            piece, dlt.at[y // 2, at(z, core), half_of(zl)], z_s.at[u], z_r.at[z, zl],
            (rep, x * 2 + y % 2, z_of[u]),
        )

    yp = in_y((y + 1) % NY)
    ym = in_y((y + NY - 1) % NY)
    other = (rep + 1 - 2 * core, tp, z)

    def unit(y_o, u, core_o):
        return dlt.at[(y_o + 2 * NY) % NY // 2, at(z_of[u], core_o)]

    def y_copy(d, k, y_o, u):
        ref = unit(y_o, u, core)
        return remote(ref, ref, y_s.at[d, k], y_r.at[d, k], (yp, ym)[d])

    def c_copy(y_o, pair, core_o):
        a = (y_o + 2 * NY) % NY // 2
        low = (core_o * 2 + (z // 2 + pair) % 2) * 2 * rows
        ref = dlt.at[a, pl.ds(pl.multiple_of(low, 16), 2 * rows)]
        return remote(ref, ref, c_s.at[a, pair], c_r.at[a, pair], other)

    def across(d, y_o, seen):
        if len(seen) >= 2:
            pair = seen[-1] // 2
            if {2 * pair, 2 * pair + 1} <= set(seen):
                c_copy(y_o, pair, core).start()

    def origin(d, hops):
        return y - hops if d == 0 else y + hops

    base = jnp.where(is_source, y // 2, (y + NY - 1) % NY // 2)
    turn = jnp.where(is_source, 1, -1)

    def ready(a):
        for pair in range(2):
            c_copy(2 * a + zl, pair, 1 - core).wait_recv()
        away = (a - x + NX) % NX

        @pl.when(away == 3)
        def _():
            x_copy(0, 1, (x + NX - 1) % NX, 1).wait_recv()

        @pl.when(away == 1)
        def _():
            x_copy(1, 1, (x + 1) % NX, 0).wait_recv()

        @pl.when(away == 2)
        def _():
            x_copy(0, 2, (x + 2) % NX, 0).wait_recv()
            x_copy(1, 2, (x + 2) % NX, 1).wait_recv()

    def products(pair):
        a0, a1 = (base, (base + NX - turn) % NX) if pair == 0 else ((base + NX + turn) % NX, (base + 2) % NX)
        ready(a0)
        ready(a1)

        def one(t, carry):
            if pair == 0:
                t_copy(1 - zl, t).wait_recv()
            at_t = pl.ds(pl.multiple_of(t * chunk, chunk), chunk)
            proj = jnp.dot(hid[a0, at_t], dlt[a0], preferred_element_type=jnp.float32)
            proj += jnp.dot(hid[a1, at_t], dlt[a1], preferred_element_type=jnp.float32)
            prod = proj * tgt[at_t].astype(jnp.float32)
            acc = score[at_t]
            for j in range(2 * width // 128):
                acc += prod[:, j * 128 : (j + 1) * 128]
            score[at_t] = acc
            return carry

        lax.fori_loop(0, 4, one, 0, unroll=2)

    @pl.when(is_source)
    def _():
        for u in (1, 2, 3):
            z_copy(u).start()
        dlt[y // 2, at(z, core), half_of(zl)] = delta
        for c in range(4):
            t_copy(zl, c).start()
        for u in range(4):
            for b in range(2):
                ref = dlt.at[y // 2, at(z_of[u], core), half_of(b)]
                arrival = remote(ref, ref, z_s.at[1], z_r.at[z_of[u], b], (rep, tp, z))
                if u == 0:
                    pl.when(b != zl)(lambda a=arrival: a.wait_recv())
                else:
                    arrival.wait_recv()
            y_copy(0, u, y, u).start()
            if u != 1:
                y_copy(1, NEAR[1].index(u), y, u).start()
        y_copy(1, 3, y, 1).start()
        for pair in range(2):
            c_copy(y, pair, core).start()
        seen = [[], []]
        for i in range(4):
            if i == 1:
                x_relay()
            for d in range(2):
                near = FAR[d][i]
                late = []
                while len(seen[d]) <= near:
                    k = len(seen[d])
                    y_copy(d, k, origin(d, 2), NEAR[d][k]).wait_recv()
                    seen[d].append(NEAR[d][k])
                    late.append(list(seen[d]))
                y_copy(d, 4 + i, origin(d, 2), NEAR[d][near]).start()
                for got in late:
                    across(d, origin(d, 2), got)
        products(0)
        for d in range(2):
            for k in (4, 5):
                y_copy(d, k, origin(d, 4), NEAR[d][FAR[d][k - 4]]).wait_recv()
            c_copy(origin(d, 4), d, core).start()
        for d in range(2):
            for k in range(8):
                y_copy(d, k, y, 0).wait_send()

    @pl.when(not_source)
    def _():
        for u in range(4):
            z_copy(u).start()
        for c in range(4):
            t_copy(zl, c).start()
        for k in range(8):
            if k == 2:
                x_relay()
            for d in range(2):
                order = NEAR[d] if k < 4 else [NEAR[d][n] for n in FAR[d]]
                y_o = origin(d, 1 if k < 4 else 3)
                y_copy(d, k, y_o, order[k % 4]).wait_recv()
                if k < 6:
                    y_copy(d, k, y_o, order[k % 4]).start()
                across(d, y_o, order[: k % 4 + 1])
            if k == 5:
                products(0)
        for d in range(2):
            for k in range(6):
                y_copy(d, k, y, 0).wait_send()
        z_copy(0).wait_send()

    products(1)

    lane = lax.broadcasted_iota(jnp.int32, (1, 128), 1)
    low = jnp.zeros((1, 128), jnp.int32)
    high = jnp.where(lane == STEPS, lengths[0], jnp.zeros((1, 128), jnp.int32))
    for k in range(STEPS):
        low = jnp.where(lane == k + 1, bounds[0, k], low)
        high = jnp.where(lane == k, jnp.minimum(bounds[0, k], lengths[0]), high)
    pos = lax.broadcasted_iota(jnp.int32, (tokens, 128), 0)
    inside = (pos >= low) & (pos < high)
    line = jnp.sum(score[...], axis=1, keepdims=True)
    sums[tp, 0:1] = 0.05 * jnp.sum(jnp.where(inside, line, 0.0), axis=0, keepdims=True)
    pending += spread(sums, tp, su_s, su_r, in_tp)
    sums_out[...] = gather(sums, su_s, su_r)

    for c in pending:
        c.wait_send()
    for c in range(4):
        t_copy(zl, c).wait_send()
    x_copy(0, 2, (x + NX - 1) % NX, 0).wait_send()
    x_copy(1, 2, (x + 1) % NX, 1).wait_send()
    for u in (1, 2, 3):
        z_copy(u).wait_send()
    for a in range(NX):
        for pair in range(2):
            c_copy(2 * a + zl, pair, core).wait_send()


def finish(total, sums, grads, master, first, second, steps_out, master_out, first_out, second_out):
    clip = 1.0 / jnp.sqrt(total[:, 0:1] + 1e-06)
    scaled = clip * grads[...]
    moment_one = 0.9 * first[...] + 0.1 * scaled
    moment_two = 0.95 * second[...] + 0.05 * scaled * scaled
    corrected = moment_one / first_fix / (jnp.sqrt(moment_two / second_fix) + 1e-08)
    old = master[...]
    master_out[...] = old - 0.002 * (corrected + 0.1 * old)
    first_out[...] = moment_one
    second_out[...] = moment_two
    steps_out[...] = sums[:, 0 : STEPS + 1]


def local(hidden_in, target_rows, grads, master, first_moment, second_moment, ref_weight, lengths, boundaries):
    tokens, width = hidden_in.shape
    rows = grads.shape[0]
    f32, bf16 = jnp.float32, jnp.bfloat16
    weight = jax.ShapeDtypeStruct(grads.shape, f32)
    line = jax.ShapeDtypeStruct((1, 128), f32)
    dma, vmem = pltpu.SemaphoreType.DMA, pltpu.VMEM
    any_space = pl.BlockSpec(memory_space=pl.ANY)
    smem = pl.BlockSpec(memory_space=pltpu.SMEM)
    in_vmem = pl.BlockSpec(memory_space=pltpu.VMEM)
    total, sums = pl.pallas_call(
        kernel,
        out_shape=(line, line),
        in_specs=[any_space] * 7 + [smem] * 2,
        out_specs=(in_vmem, in_vmem),
        scratch_shapes=[
            vmem((NX, tokens, width), bf16),
            vmem((tokens, 2 * width), bf16),
            vmem((NX, 8 * rows, 2 * width), bf16),
            vmem((rows, width), bf16),
            *[vmem((rows, width), f32)] * 4,
            vmem((rows, width), bf16),
            *[vmem((8, 8, 128), f32)] * 4,
            vmem((tokens, 128), f32),
            dma((7,)),
            *[dma((7,)), dma(())] * 4,
            dma((2, 3)), dma((2, 3)),
            dma((4,)), dma((4,)),
            dma((4,)), dma((4, 2)),
            dma((2, 8)), dma((2, 8)),
            dma((4, 2)), dma((4, 2)),
        ],
        compiler_params=pltpu.CompilerParams(
            collective_id=0, has_side_effects=True, vmem_limit_bytes=63 * 2**20
        ),
        cost_estimate=pl.CostEstimate(
            flops=2 * tokens * 8 * width * width, bytes_accessed=6 * 2**20, transcendentals=0
        ),
    )(hidden_in, target_rows, grads, master, first_moment, second_moment, ref_weight, lengths, boundaries)
    return tuple(
        pl.pallas_call(
            finish,
            out_shape=(jax.ShapeDtypeStruct((1, STEPS + 1), f32), weight, weight, weight),
            in_specs=[in_vmem] * 6,
            out_specs=(in_vmem,) * 4,
        )(total, sums, grads, master, first_moment, second_moment)
    )


def solution(mesh):
    block = P(("rep", "fsdp"), "tp")
    return jax.shard_map(
        local,
        mesh=mesh,
        in_specs=(block,) * 7 + (P(("rep", "fsdp")), P(("rep", "fsdp"), None)),
        out_specs=(P(("rep", "fsdp"), None), block, block, block),
        check_vma=False,
    )
```

```python
import functools

import jax
import jax.numpy as jnp
from jax import lax
from jax.experimental import pallas as pl
from jax.experimental.pallas import tpu as pltpu
from jax.sharding import PartitionSpec as P

MESH = pl.DeviceIdType.MESH
STEPS = 8
NX, NY, NZ = 4, 8, 4
NEAR = ((0, 1, 2, 3), (0, 2, 3, 1))
FAR = ((0, 1, 2, 3), (1, 2, 0, 3))


first_fix = 1.0 - (0.9**10) ** 10
second_fix = 1.0 - (0.95**10) ** 10


def kernel(
    hidden, target, grads, master, first, second, refw, lengths, bounds,
    total_out, sums_out,
    hid, tgt, dlt, piece, g_v, ma_v, m1_v, m2_v, rw_v,
    na, nb, nc, sums, score,
    local_sem,
    na_s, na_r, nb_s, nb_r, nc_s, nc_r, su_s, su_r,
    x_s, x_r, t_s, t_r, z_s, z_r, y_s, y_r, c_s, c_r,
):
    rep, tp, z = lax.axis_index("rep"), lax.axis_index("tp"), lax.axis_index("fsdp")
    y, core = rep // 2, rep % 2
    x, zl = tp // 2, tp % 2
    ntp = 2 * NX
    rows = piece.shape[0]
    tokens = hid.shape[1]
    half = tokens // 2
    chunk = tokens // 4
    is_source = zl == y % 2
    not_source = jnp.logical_not(is_source)

    def remote(src, dst, send, recv, device):
        return pltpu.make_async_remote_copy(
            src_ref=src, dst_ref=dst, send_sem=send, recv_sem=recv,
            device_id=device, device_id_type=MESH,
        )

    width = piece.shape[1]

    def half_of(b):
        return pl.ds(pl.multiple_of(b * width, 128), width)

    loads = [
        pltpu.make_async_copy(a, b, local_sem.at[i])
        for i, (a, b) in enumerate((
            (grads, g_v),
            (hidden, hid.at[x]),
            (first, m1_v),
            (second, m2_v),
            (master, ma_v),
            (refw, rw_v),
            (target, tgt.at[:, half_of(zl)]),
        ))
    ]
    for c in loads:
        c.start()

    barrier = pltpu.get_barrier_semaphore()

    def in_tp(j):
        return rep, j, z

    def in_y(j):
        return j * 2 + core, tp, z

    def in_cz(j):
        return y * 2 + j // NZ, tp, j % NZ

    def greet(device):
        pl.semaphore_signal(barrier, inc=1, device_id=device, device_id_type=MESH)

    cz = core * NZ + z
    for r in range(1, 8):
        greet(in_tp((tp + r) % 8))
        greet(in_y((y + r) % 8))
        greet(in_cz((cz + r) % 8))
    for r in range(1, NZ):
        greet((rep, x * 2 + 1 - zl, (z + r) % NZ))

    loads[0].wait()
    g = g_v[...]
    part = jnp.sum(jnp.sum(g * g, axis=0, keepdims=True), axis=1, keepdims=True)
    na[tp, 0:1] = jnp.broadcast_to(part, (1, 128))
    pl.semaphore_wait(barrier, 3 * 7 + NZ - 1)

    def spread(buf, me, sends, recv, device_of):
        out = []
        row = buf.at[me, pl.ds(0, 1)]
        for r in range(1, 8):
            c = remote(row, row, sends.at[r - 1], recv, device_of((me + r) % 8))
            c.start()
            out.append(c)
        return out

    def gather(buf, sends, recv):
        part = buf.at[pl.ds(0, 7), pl.ds(0, 1)]
        remote(part, part, sends.at[0], recv, (rep, tp, z)).wait_recv()
        return jnp.sum(buf[:, 0:1, :], axis=0)

    xp = (rep, ((x + 1) % NX) * 2 + zl, z)
    xm = (rep, ((x + NX - 1) % NX) * 2 + zl, z)

    def x_copy(d, k, owner, c):
        ref = hid.at[owner, pl.ds(c * half, half)]
        return remote(ref, ref, x_s.at[d, k], x_r.at[d, k], (xp, xm)[d])

    def x_relay():
        x_copy(0, 0, (x + NX - 1) % NX, 0).wait_recv()
        x_copy(0, 2, (x + NX - 1) % NX, 0).start()
        x_copy(1, 0, (x + 1) % NX, 1).wait_recv()
        x_copy(1, 2, (x + 1) % NX, 1).start()

    def t_copy(owner, c):
        ref = tgt.at[pl.ds(pl.multiple_of(c * chunk, 16), chunk), half_of(owner)]
        return remote(ref, ref, t_s.at[c], t_r.at[c], (rep, x * 2 + 1 - zl, z))

    pending = []

    def start(copy):
        copy.start()
        pending.append(copy)

    pending += spread(na, tp, na_s, na_r, in_tp)
    loads[6].wait()
    nb[y, 0:1] = gather(na, na_s, na_r)
    pending += spread(nb, y, nb_s, nb_r, in_y)

    loads[1].wait()
    for i in range(2):
        start(x_copy(0, i, x, i))
        start(x_copy(1, i, x, 1 - i))

    nc[cz, 0:1] = gather(nb, nb_s, nb_r)
    pending += spread(nc, cz, nc_s, nc_r, in_cz)
    score[...] = jnp.zeros_like(score)
    for c in loads[2:6]:
        c.wait()
    total = gather(nc, nc_s, nc_r)
    total_out[...] = total
    total = total[:, 0:1]
    clip = 1.0 / jnp.sqrt(total + 1e-06)

    scaled = clip * g_v[...]
    moment_one = 0.9 * m1_v[...] + 0.1 * scaled
    moment_two = 0.95 * m2_v[...] + 0.05 * scaled * scaled
    corrected = moment_one / first_fix / (jnp.sqrt(moment_two / second_fix) + 1e-08)
    old = ma_v[...]
    master_new = old - 0.002 * (corrected + 0.1 * old)
    delta = (master_new - rw_v[...].astype(jnp.float32)).astype(jnp.bfloat16)
    piece[...] = delta

    def at(z_o, core_o):
        return pl.ds(pl.multiple_of((core_o * NZ + z_o) * rows, 16), rows)

    z_of = (z, z + 1 - 2 * (z % 2), NZ - 1 - z, (z + 2) % NZ)

    def z_copy(u):
        return remote(
            piece, dlt.at[y // 2, at(z, core), half_of(zl)], z_s.at[u], z_r.at[z, zl],
            (rep, x * 2 + y % 2, z_of[u]),
        )

    yp = in_y((y + 1) % NY)
    ym = in_y((y + NY - 1) % NY)
    other = (rep + 1 - 2 * core, tp, z)

    def unit(y_o, u, core_o):
        return dlt.at[(y_o + 2 * NY) % NY // 2, at(z_of[u], core_o)]

    def y_copy(d, k, y_o, u):
        ref = unit(y_o, u, core)
        return remote(ref, ref, y_s.at[d, k], y_r.at[d, k], (yp, ym)[d])

    def c_copy(y_o, pair, core_o):
        a = (y_o + 2 * NY) % NY // 2
        low = (core_o * 2 + (z // 2 + pair) % 2) * 2 * rows
        ref = dlt.at[a, pl.ds(pl.multiple_of(low, 16), 2 * rows)]
        return remote(ref, ref, c_s.at[a, pair], c_r.at[a, pair], other)

    def across(d, y_o, seen):
        if len(seen) >= 2:
            pair = seen[-1] // 2
            if {2 * pair, 2 * pair + 1} <= set(seen):
                c_copy(y_o, pair, core).start()

    def origin(d, hops):
        return y - hops if d == 0 else y + hops

    base = jnp.where(is_source, y // 2, (y + NY - 1) % NY // 2)
    turn = jnp.where(is_source, 1, -1)

    def ready(a):
        for pair in range(2):
            c_copy(2 * a + zl, pair, 1 - core).wait_recv()
        away = (a - x + NX) % NX

        @pl.when(away == 3)
        def _():
            x_copy(0, 1, (x + NX - 1) % NX, 1).wait_recv()

        @pl.when(away == 1)
        def _():
            x_copy(1, 1, (x + 1) % NX, 0).wait_recv()

        @pl.when(away == 2)
        def _():
            x_copy(0, 2, (x + 2) % NX, 0).wait_recv()
            x_copy(1, 2, (x + 2) % NX, 1).wait_recv()

    def products(pair):
        a0, a1 = (base, (base + NX - turn) % NX) if pair == 0 else ((base + NX + turn) % NX, (base + 2) % NX)
        ready(a0)
        ready(a1)

        def one(t, carry):
            if pair == 0:
                t_copy(1 - zl, t).wait_recv()
            at_t = pl.ds(pl.multiple_of(t * chunk, chunk), chunk)
            proj = jnp.dot(hid[a0, at_t], dlt[a0], preferred_element_type=jnp.float32)
            proj += jnp.dot(hid[a1, at_t], dlt[a1], preferred_element_type=jnp.float32)
            prod = proj * tgt[at_t].astype(jnp.float32)
            acc = score[at_t]
            for j in range(2 * width // 128):
                acc += prod[:, j * 128 : (j + 1) * 128]
            score[at_t] = acc
            return carry

        lax.fori_loop(0, 4, one, 0, unroll=2)

    @pl.when(is_source)
    def _():
        for u in (1, 2, 3):
            z_copy(u).start()
        dlt[y // 2, at(z, core), half_of(zl)] = delta
        for c in range(4):
            t_copy(zl, c).start()
        for u in range(4):
            for b in range(2):
                ref = dlt.at[y // 2, at(z_of[u], core), half_of(b)]
                arrival = remote(ref, ref, z_s.at[1], z_r.at[z_of[u], b], (rep, tp, z))
                if u == 0:
                    pl.when(b != zl)(lambda a=arrival: a.wait_recv())
                else:
                    arrival.wait_recv()
            y_copy(0, u, y, u).start()
            if u != 1:
                y_copy(1, NEAR[1].index(u), y, u).start()
        y_copy(1, 3, y, 1).start()
        for pair in range(2):
            c_copy(y, pair, core).start()
        seen = [[], []]
        for i in range(4):
            if i == 1:
                x_relay()
            for d in range(2):
                near = FAR[d][i]
                late = []
                while len(seen[d]) <= near:
                    k = len(seen[d])
                    y_copy(d, k, origin(d, 2), NEAR[d][k]).wait_recv()
                    seen[d].append(NEAR[d][k])
                    late.append(list(seen[d]))
                y_copy(d, 4 + i, origin(d, 2), NEAR[d][near]).start()
                for got in late:
                    across(d, origin(d, 2), got)
        products(0)
        for d in range(2):
            for k in (4, 5):
                y_copy(d, k, origin(d, 4), NEAR[d][FAR[d][k - 4]]).wait_recv()
            c_copy(origin(d, 4), d, core).start()
        for d in range(2):
            for k in range(8):
                y_copy(d, k, y, 0).wait_send()

    @pl.when(not_source)
    def _():
        for u in range(4):
            z_copy(u).start()
        for c in range(4):
            t_copy(zl, c).start()
        for k in range(8):
            if k == 2:
                x_relay()
            for d in range(2):
                order = NEAR[d] if k < 4 else [NEAR[d][n] for n in FAR[d]]
                y_o = origin(d, 1 if k < 4 else 3)
                y_copy(d, k, y_o, order[k % 4]).wait_recv()
                if k < 6:
                    y_copy(d, k, y_o, order[k % 4]).start()
                across(d, y_o, order[: k % 4 + 1])
            if k == 5:
                products(0)
        for d in range(2):
            for k in range(6):
                y_copy(d, k, y, 0).wait_send()
        z_copy(0).wait_send()

    products(1)

    lane = lax.broadcasted_iota(jnp.int32, (1, 128), 1)
    low = jnp.zeros((1, 128), jnp.int32)
    high = jnp.where(lane == STEPS, lengths[0], jnp.zeros((1, 128), jnp.int32))
    for k in range(STEPS):
        low = jnp.where(lane == k + 1, bounds[0, k], low)
        high = jnp.where(lane == k, jnp.minimum(bounds[0, k], lengths[0]), high)
    pos = lax.broadcasted_iota(jnp.int32, (tokens, 128), 0)
    inside = (pos >= low) & (pos < high)
    line = jnp.sum(score[...], axis=1, keepdims=True)
    sums[tp, 0:1] = 0.05 * jnp.sum(jnp.where(inside, line, 0.0), axis=0, keepdims=True)
    last = spread(sums, tp, su_s, su_r, in_tp)

    for c in pending:
        c.wait_send()
    for c in range(4):
        t_copy(zl, c).wait_send()
    x_copy(0, 2, (x + NX - 1) % NX, 0).wait_send()
    x_copy(1, 2, (x + 1) % NX, 1).wait_send()
    for u in (1, 2, 3):
        z_copy(u).wait_send()
    for a in range(NX):
        for pair in range(2):
            c_copy(2 * a + zl, pair, core).wait_send()
    sums_out[...] = gather(sums, su_s, su_r)
    for c in last:
        c.wait_send()


def finish(total, sums, grads, master, first, second, steps_out, master_out, first_out, second_out):
    clip = 1.0 / jnp.sqrt(total[:, 0:1] + 1e-06)
    scaled = clip * grads[...]
    moment_one = 0.9 * first[...] + 0.1 * scaled
    moment_two = 0.95 * second[...] + 0.05 * scaled * scaled
    corrected = moment_one / first_fix / (jnp.sqrt(moment_two / second_fix) + 1e-08)
    old = master[...]
    master_out[...] = old - 0.002 * (corrected + 0.1 * old)
    first_out[...] = moment_one
    second_out[...] = moment_two
    steps_out[...] = sums[:, 0 : STEPS + 1]


def local(hidden_in, target_rows, grads, master, first_moment, second_moment, ref_weight, lengths, boundaries):
    tokens, width = hidden_in.shape
    rows = grads.shape[0]
    f32, bf16 = jnp.float32, jnp.bfloat16
    weight = jax.ShapeDtypeStruct(grads.shape, f32)
    line = jax.ShapeDtypeStruct((1, 128), f32)
    dma, vmem = pltpu.SemaphoreType.DMA, pltpu.VMEM
    any_space = pl.BlockSpec(memory_space=pl.ANY)
    smem = pl.BlockSpec(memory_space=pltpu.SMEM)
    in_vmem = pl.BlockSpec(memory_space=pltpu.VMEM)
    total, sums = pl.pallas_call(
        kernel,
        out_shape=(line, line),
        in_specs=[any_space] * 7 + [smem] * 2,
        out_specs=(in_vmem, in_vmem),
        scratch_shapes=[
            vmem((NX, tokens, width), bf16),
            vmem((tokens, 2 * width), bf16),
            vmem((NX, 8 * rows, 2 * width), bf16),
            vmem((rows, width), bf16),
            *[vmem((rows, width), f32)] * 4,
            vmem((rows, width), bf16),
            *[vmem((8, 8, 128), f32)] * 4,
            vmem((tokens, 128), f32),
            dma((7,)),
            *[dma((7,)), dma(())] * 4,
            dma((2, 3)), dma((2, 3)),
            dma((4,)), dma((4,)),
            dma((4,)), dma((4, 2)),
            dma((2, 8)), dma((2, 8)),
            dma((4, 2)), dma((4, 2)),
        ],
        compiler_params=pltpu.CompilerParams(
            collective_id=0, has_side_effects=True, vmem_limit_bytes=63 * 2**20
        ),
        cost_estimate=pl.CostEstimate(
            flops=2 * tokens * 8 * width * width, bytes_accessed=6 * 2**20, transcendentals=0
        ),
    )(hidden_in, target_rows, grads, master, first_moment, second_moment, ref_weight, lengths, boundaries)
    return tuple(
        pl.pallas_call(
            finish,
            out_shape=(jax.ShapeDtypeStruct((1, STEPS + 1), f32), weight, weight, weight),
            in_specs=[in_vmem] * 6,
            out_specs=(in_vmem,) * 4,
        )(total, sums, grads, master, first_moment, second_moment)
    )


def solution(mesh):
    block = P(("rep", "fsdp"), "tp")
    return jax.shard_map(
        local,
        mesh=mesh,
        in_specs=(block,) * 7 + (P(("rep", "fsdp")), P(("rep", "fsdp"), None)),
        out_specs=(P(("rep", "fsdp"), None), block, block, block),
        check_vma=False,
    )
```
